32 devices in a mesh: ta: 4 (over y, x), gz: 4 (over z), col: 2 (over core).
Axes of the slice: x: 2, y: 2, z: 4, core: 2. Of those that a mesh axis runs over, the one named last changes fastest.
Arguments:
- right_sides: bfloat16 [4, 2, 2, 4, 4, 8, 384], P('col', None, None, 'ta', 'gz'), may hold values from -6 to 6
- null_vectors: bfloat16 [32, 2, 2, 4, 4, 8, 384], P(None, None, None, 'ta', 'gz'), may hold values from -0.3125 to 0.3125
- coarse_op: bfloat16 [4, 4, 1, 2, 9, 64, 128], P('ta', 'gz'), may hold values from -0.1875 to 0.1875
Outputs:
- correction: float32 [4, 2, 2, 4, 4, 8, 384], P('col', None, None, 'ta', 'gz')
The draws below stay inside these ranges and needn't reach their ends.
All inputs are finite; a program needn't handle non-finite values.
Results may differ from the reference program's by a relative error of at most 0.0054.
Values may be sent and summed in bfloat16 or wider, within the bound.
A program may use at most 64 MiB of HBM per device.

```python
import jax
import jax.numpy as jnp
from jax import lax

RHS = 4
NVEC = 32
NDOF = 64
CY = 2
CX = 4
CZ = 4
CT = 1
LT = 4


def shard_levels(stream_key, shape, split, smallest, largest):
    loudness = 1.0
    for position, blocks in split:
        draws = jax.random.uniform(jax.random.fold_in(jax.random.fold_in(stream_key, 6), position), (blocks,), jnp.float32, smallest / len(split), largest / len(split))
        loudness = loudness * jnp.repeat(jnp.exp(draws), shape[position] // blocks).reshape((-1,) + (1,) * (len(shape) - 1 - position))
    return loudness


def centred(rng, dims, deviation, limit, cuts=(), held_as=jnp.bfloat16):
    entries = jax.random.normal(rng, dims, jnp.float32) * deviation
    if len(cuts) > 0:
        entries = shard_levels(rng, dims, cuts, -0.22, 0.18) * entries
    return jnp.clip(entries, min=-limit, max=limit).astype(held_as)


def setup_inputs(seed: int = 0) -> dict:
    seeds = jax.random.split(jax.random.key(seed), 4)
    right_sides = centred(seeds[0], (RHS, 2, 2, LT, CZ, CX * CY, 384), 1.0, 6.0, ((0, 2), (3, 4), (4, 4)))
    null_vectors = centred(seeds[1], (NVEC, 2, 2, LT, CZ, CX * CY, 384), 0.05, 0.3125, ((3, 4), (4, 4)))
    coarse_op = centred(seeds[2], (CX, CZ, CT, CY, 9, NDOF, 2 * NDOF), (18 * NDOF) ** -0.5, 0.1875, ((0, 4), (1, 4)))
    return {"right_sides": right_sides, "null_vectors": null_vectors, "coarse_op": coarse_op}


def restrict_slice(vectors, fields):
    vectors = vectors.astype(jnp.float32)
    fields = fields.astype(jnp.float32)
    stacked = jnp.stack([fields, jnp.stack([fields[:, 1], -fields[:, 0]], axis=1)], axis=1)
    products = jnp.einsum("kphwbn,rQphwbn->wbrQhk", vectors, stacked)
    return products.reshape(CZ, CX * CY, RHS, 2 * NDOF)


def apply_coarse(coarse, coarse_op):
    shifted = jnp.stack([coarse, jnp.roll(coarse, -1, 0), jnp.roll(coarse, 1, 0),
                         jnp.roll(coarse, -1, 3), jnp.roll(coarse, 1, 3),
                         jnp.roll(coarse, -1, 1), jnp.roll(coarse, 1, 1),
                         jnp.roll(coarse, -1, 2), jnp.roll(coarse, 1, 2)])
    real_part = shifted[..., :NDOF]
    imag_part = shifted[..., NDOF:]
    stacked = jnp.stack([jnp.concatenate([real_part, -imag_part], axis=-1),
                         jnp.concatenate([imag_part, real_part], axis=-1)], axis=-2)

    def one_plane(pair):
        blocks, values = pair
        return jnp.einsum("ztymoc,mztyrsc->ztyrso", blocks.astype(jnp.float32), values.astype(jnp.float32))

    result = lax.map(one_plane, (coarse_op, jnp.moveaxis(stacked, 1, 0)))
    return result.reshape(coarse.shape)


def reference(right_sides, null_vectors, coarse_op):
    def restrict_one(index):
        vectors = lax.dynamic_index_in_dim(null_vectors, index, 3, keepdims=False)
        fields = lax.dynamic_index_in_dim(right_sides, index, 3, keepdims=False)
        return restrict_slice(vectors, fields)

    partials = lax.map(restrict_one, jnp.arange(LT, dtype=jnp.int32))
    summed = partials.reshape(CT, 4, CZ, CX, CY, RHS, 2 * NDOF).sum(axis=1)
    coarse = jnp.transpose(summed, (2, 1, 0, 3, 4, 5)).astype(jnp.bfloat16)
    applied = apply_coarse(coarse, coarse_op).astype(jnp.bfloat16)
    twice = apply_coarse(applied, coarse_op).astype(jnp.bfloat16)

    def expand_one(index):
        vectors = lax.dynamic_index_in_dim(null_vectors, index, 3, keepdims=False).astype(jnp.float32)
        coarse_slice = lax.dynamic_index_in_dim(twice, index // 4, 2, keepdims=False)
        arranged = jnp.transpose(coarse_slice, (1, 0, 2, 3, 4)).reshape(CZ, CX * CY, RHS, 2, 2, NVEC)
        arranged = arranged.astype(jnp.float32)
        real_part = arranged[:, :, :, 0]
        imag_part = arranged[:, :, :, 1]
        mixing = jnp.stack([jnp.stack([real_part, -imag_part], axis=3),
                            jnp.stack([imag_part, real_part], axis=3)], axis=3)
        return jnp.einsum("kphwbn,wbrPphk->rPhwbn", vectors, mixing)

    expanded = lax.map(expand_one, jnp.arange(LT, dtype=jnp.int32))
    return jnp.moveaxis(expanded, 0, 3)
```

```python
import functools

import jax
import jax.numpy as jnp
from jax import lax
from jax.experimental import pallas as pl
from jax.experimental.pallas import tpu as pltpu
from jax.sharding import PartitionSpec as P

TSITES = 4
MESH = pl.DeviceIdType.MESH
F32 = jnp.float32
BF16 = jnp.bfloat16
NN = (((1,), (0,)), ((), ()))
NT = (((1,), (1,)), ((), ()))


def dot(a, b, dims):
    return lax.dot_general(a, b, dims, preferred_element_type=F32)


def same_block(rows, lanes, row_period):
    i = lax.broadcasted_iota(jnp.int32, (rows, lanes), 0)
    j = lax.broadcasted_iota(jnp.int32, (rows, lanes), 1)
    return ((i ^ j) & (row_period - 1)) == 0


def kernel(
    dims, fields_hbm, vectors_hbm, ops_hbm, out_ref,
    fields, vectors, ops, fold, spread, ext, matrix, recv, recvz, mine, halo, final, gath,
    load_sem, send1, recv1, sendz, recvz_sem, send2, recv2, send3, recv3,
):
    nx, nz, nt, ny, nr, nv, nb, chunk = dims
    me = lax.axis_index("ta")
    z = lax.axis_index("gz")
    col = lax.axis_index("col")
    up = lax.rem(z + 1, nz)
    down = lax.rem(z + nz - 1, nz)
    shift = nb.bit_length() - 1
    vec_rows = vectors.shape[0]
    rows = fields.shape[0]

    load_f = pltpu.make_async_copy(fields_hbm, fields, load_sem.at[0])
    load_v = pltpu.make_async_copy(vectors_hbm, vectors, load_sem.at[1])
    load_o = pltpu.make_async_copy(ops_hbm, ops, load_sem.at[2])
    load_f.start()
    load_v.start()
    load_o.start()

    barrier = pltpu.get_barrier_semaphore()
    for d in range(nx):
        other = lax.rem(me + d, nx)
        for plane in (up, down) if d == 0 else (up, down, z):
            pl.semaphore_signal(
                barrier, inc=1, device_id=(other, plane, col), device_id_type=MESH
            )

    i = lax.broadcasted_iota(jnp.int32, (vec_rows, 128), 0)
    j = lax.broadcasted_iota(jnp.int32, (vec_rows, 128), 1)
    lane_of = ((i >> shift) & 3) * nv + (i >> (shift + 2))
    fold[...] = jnp.where(lane_of == j, 1.0, 0.0).astype(BF16)
    i = lax.broadcasted_iota(jnp.int32, (128, vec_rows), 1)
    j = lax.broadcasted_iota(jnp.int32, (128, vec_rows), 0)
    lane_of = ((i >> shift) & 3) * nv + (i >> (shift + 2))
    spread[...] = jnp.where(lane_of == j, 1.0, 0.0).astype(BF16)

    load_f.wait()
    load_v.wait()

    mask = same_block(rows, chunk, 2 * nb)
    left = fields[...]
    total = jnp.zeros((rows, 128), F32)
    for c in range(vec_rows // chunk):
        part = pl.ds(c * chunk, chunk)
        grid = jnp.where(mask, dot(left, vectors[part, :], NT), 0.0)
        high = grid.astype(BF16)
        low = (grid - high.astype(F32)).astype(BF16)
        both = dot(jnp.concatenate([high, low], axis=0), fold[part, :], NN)
        total = total + (both[:rows] + both[rows:])
    lane = lax.broadcasted_iota(jnp.int32, (nb, 128), 1)
    sign = jnp.where(lane < 64, 1.0, -1.0)
    for r in range(nr):
        block = [total[(r * 4 + q) * nb:(r * 4 + q + 1) * nb] for q in range(4)]
        coarse = sign * (block[0] + block[1]) + pltpu.roll(block[2] + block[3], 64, 1)
        for x in range(nx):
            ext[x + 1, r * ny:(r + 1) * ny, :] = coarse[x * ny:(x + 1) * ny]
        ext[0, r * ny:(r + 1) * ny, :] = coarse[(nx - 1) * ny:]
        ext[nx + 1, r * ny:(r + 1) * ny, :] = coarse[:ny]

    pl.semaphore_wait(barrier, 3 * nx - 1)
    sends = []
    for d in range(nx):
        other = lax.rem(me + d, nx)
        for side, plane in ((1, up), (0, down)):
            sends.append(
                pltpu.make_async_remote_copy(
                    src_ref=ext.at[other + 1],
                    dst_ref=recvz.at[side, me],
                    send_sem=sendz.at[side, d],
                    recv_sem=recvz_sem.at[side, d],
                    device_id=(other, plane, col),
                    device_id_type=MESH,
                )
            )
            sends[-1].start()
        if d > 0:
            sends.append(
                pltpu.make_async_remote_copy(
                    src_ref=ext.at[pl.ds(other, 3)],
                    dst_ref=recv.at[me],
                    send_sem=send1.at[d],
                    recv_sem=recv1.at[d],
                    device_id=(other, z, col),
                    device_id_type=MESH,
                )
            )
            sends[-1].start()
    recv[pl.ds(me, 1)] = ext[pl.ds(me, 3)][None]

    load_o.wait()
    lane = lax.broadcasted_iota(jnp.int32, (64, 128), 1)
    sign64 = jnp.where(lane < 64, 1.0, -1.0)
    for t in range(nt):
        for y in range(ny):
            for m in range(9):
                a = ops[t * ny + y, m].astype(F32)
                cols = pl.ds(m * 128, 128)
                matrix[t, y * 128:y * 128 + 64, cols] = (a * sign64).astype(BF16)
                matrix[t, y * 128 + 64:y * 128 + 128, cols] = pltpu.roll(a, 64, 1).astype(BF16)

    site = lax.broadcasted_iota(jnp.int32, (nr * ny, 128), 0)

    def roll_y(v, step):
        pieces = []
        for r in range(nr):
            for y in range(ny):
                row = r * ny + (y + step) % ny
                pieces.append(v[row:row + 1])
        return jnp.concatenate(pieces, axis=0)

    def apply(own, xp, xm, zp, zm):
        results = []
        for t in range(nt):
            v = own[t]
            yp, ym = roll_y(v, 1), roll_y(v, -1)
            around = jnp.concatenate(
                [v, xp[t], xm[t], yp, ym, zp[t], zm[t], own[(t + 1) % nt], own[(t - 1) % nt]],
                axis=1,
            )
            product = dot(around.astype(BF16), matrix[t], NT)
            value = product[:, :128]
            for y in range(1, ny):
                value = jnp.where(
                    lax.rem(site, ny) == y, product[:, y * 128:(y + 1) * 128], value
                )
            results.append(value.astype(BF16).astype(F32))
        return results

    for copy in sends:
        copy.wait_recv()

    def summed(load):
        results = []
        for t in range(nt):
            value = load(t * TSITES)
            for s in range(1, TSITES):
                value = value + load(t * TSITES + s)
            results.append(value.astype(BF16).astype(F32))
        return results

    applied = apply(
        summed(lambda s: recv[s, 1]),
        summed(lambda s: recv[s, 2]),
        summed(lambda s: recv[s, 0]),
        summed(lambda s: recvz[0, s]),
        summed(lambda s: recvz[1, s]),
    )
    for t in range(nt):
        mine[t] = applied[t]

    right = lax.rem(me + 1, nx)
    left_x = lax.rem(me + nx - 1, nx)
    places = ((1, (right, z)), (0, (left_x, z)), (3, (me, up)), (2, (me, down)))
    round2 = []
    for slot, place in places:
        round2.append(
            pltpu.make_async_remote_copy(
                src_ref=mine,
                dst_ref=halo.at[slot],
                send_sem=send2.at[slot],
                recv_sem=recv2.at[slot],
                device_id=place + (col,),
                device_id_type=MESH,
            )
        )
        round2[-1].start()
    for copy in sends:
        copy.wait_send()
    for copy in round2:
        copy.wait_recv()
    twice = apply(
        applied, *[[halo[slot, t] for t in range(nt)] for slot in range(4)]
    )
    for t in range(nt):
        final[t] = twice[t]

    round3 = []
    for d in range(1, nx):
        other = lax.rem(me + d, nx)
        round3.append(
            pltpu.make_async_remote_copy(
                src_ref=final.at[other // TSITES],
                dst_ref=gath.at[me],
                send_sem=send3.at[d],
                recv_sem=recv3.at[d],
                device_id=(other, z, col),
                device_id_type=MESH,
            )
        )
        round3[-1].start()
    gath[pl.ds(me, 1)] = final[pl.ds(me // TSITES, 1)]
    for copy in round2:
        copy.wait_send()
    for copy in round3:
        copy.wait_recv()

    pieces = []
    for r in range(nr):
        row = jnp.concatenate([gath[x, r * ny:(r + 1) * ny, :] for x in range(nx)], axis=0)
        real = sign * row
        imag = pltpu.roll(row, 64, 1)
        pieces += [real, real, imag, imag]
    mixing = jnp.concatenate(pieces, axis=0).astype(BF16)
    result = None
    for c in range(vec_rows // chunk):
        part = pl.ds(c * chunk, chunk)
        weights = jnp.where(mask, dot(mixing, spread[:, part], NN), 0.0).astype(BF16)
        term = dot(weights, vectors[part, :], NN)
        result = term if result is None else result + term
    out_ref[...] = result
    for copy in round3:
        copy.wait_send()


def per_device(right_sides, null_vectors, coarse_op):
    nx = lax.axis_size("ta")
    nz = lax.axis_size("gz")
    nt, ny = coarse_op.shape[2:4]
    nr = right_sides.shape[0]
    nv = null_vectors.shape[0]
    nb, width = null_vectors.shape[-2:]
    vec_rows = nv * 4 * nb
    rows = nr * 4 * nb
    message = (nr * ny, 128)
    dma = pltpu.SemaphoreType.DMA
    out = pl.pallas_call(
        functools.partial(kernel, (nx, nz, nt, ny, nr, nv, nb, min(vec_rows, 1024))),
        out_shape=jax.ShapeDtypeStruct((rows, width), F32),
        in_specs=[pl.BlockSpec(memory_space=pl.ANY)] * 3,
        out_specs=pl.BlockSpec(memory_space=pltpu.VMEM),
        scratch_shapes=[
            pltpu.VMEM((rows, width), BF16),
            pltpu.VMEM((vec_rows, width), BF16),
            pltpu.VMEM((nt * ny, 9, 64, 128), BF16),
            pltpu.VMEM((vec_rows, 128), BF16),
            pltpu.VMEM((128, vec_rows), BF16),
            pltpu.VMEM((nx + 2,) + message, F32),
            pltpu.VMEM((nt, ny * 128, 9 * 128), BF16),
            pltpu.VMEM((nx, 3) + message, F32),
            pltpu.VMEM((2, nx) + message, F32),
            pltpu.VMEM((nt,) + message, F32),
            pltpu.VMEM((4, nt) + message, F32),
            pltpu.VMEM((nt,) + message, F32),
            pltpu.VMEM((nx,) + message, F32),
            dma((3,)),
            dma((nx,)),
            dma((nx,)),
            dma((2, nx)),
            dma((2, nx)),
            dma((4,)),
            dma((4,)),
            dma((nx,)),
            dma((nx,)),
        ],
        compiler_params=pltpu.CompilerParams(
            collective_id=0, has_side_effects=True, vmem_limit_bytes=40 * 1024 * 1024
        ),
    )(
        right_sides.reshape(rows, width),
        null_vectors.reshape(vec_rows, width),
        coarse_op.reshape((nt * ny,) + coarse_op.shape[4:]),
    )
    return out.reshape(right_sides.shape)


def solution(mesh):
    return jax.shard_map(
        per_device,
        mesh=mesh,
        in_specs=(
            P("col", None, None, "ta", "gz", None, None),
            P(None, None, None, "ta", "gz", None, None),
            P("ta", "gz", None, None, None, None, None),
        ),
        out_specs=P("col", None, None, "ta", "gz", None, None),
        check_vma=False,
    )
```

```python
import functools

import jax
import jax.numpy as jnp
from jax import lax
from jax.experimental import pallas as pl
from jax.experimental.pallas import tpu as pltpu
from jax.sharding import PartitionSpec as P

TSITES = 4
MESH = pl.DeviceIdType.MESH
F32 = jnp.float32
BF16 = jnp.bfloat16
NN = (((1,), (0,)), ((), ()))
NT = (((1,), (1,)), ((), ()))
ORDER = (0, 3, 4, 7, 8, 1, 2, 5, 6)


def dot(a, b, dims):
    return lax.dot_general(a, b, dims, preferred_element_type=F32)


def same_block(rows, lanes, row_period):
    i = lax.broadcasted_iota(jnp.int32, (rows, lanes), 0)
    j = lax.broadcasted_iota(jnp.int32, (rows, lanes), 1)
    return ((i ^ j) & (row_period - 1)) == 0


def kernel(
    dims, fields_hbm, vectors_hbm, ops_hbm, out_ref,
    fields, vectors, ops, fold, ext, matrix, recv, recvz, mine, halo, final, gath, spread,
    load_sem, send1, recv1, sendz, recvz_sem, send2, recv2, send3, recv3,
):
    nx, nz, nt, ny, nr, nv, nb, chunk = dims
    me = lax.axis_index("ta")
    z = lax.axis_index("gz")
    col = lax.axis_index("col")
    up = lax.rem(z + 1, nz)
    down = lax.rem(z + nz - 1, nz)
    shift = nb.bit_length() - 1
    vec_rows = vectors.shape[0]
    rows = fields.shape[0]

    load_f = pltpu.make_async_copy(fields_hbm, fields, load_sem.at[0])
    pieces = [pl.ds(c * chunk, chunk) for c in range(vectors.shape[0] // chunk)]
    load_v = [
        pltpu.make_async_copy(vectors_hbm.at[part], vectors.at[part], load_sem.at[2 + c])
        for c, part in enumerate(pieces)
    ]
    load_o = pltpu.make_async_copy(ops_hbm, ops, load_sem.at[1])
    load_f.start()
    for load in load_v:
        load.start()
    load_o.start()

    barrier = pltpu.get_barrier_semaphore()
    for d in range(nx):
        other = lax.rem(me + d, nx)
        for plane in (up, down) if d == 0 else (up, down, z):
            pl.semaphore_signal(
                barrier, inc=1, device_id=(other, plane, col), device_id_type=MESH
            )

    i = lax.broadcasted_iota(jnp.int32, (vec_rows, 128), 0)
    j = lax.broadcasted_iota(jnp.int32, (vec_rows, 128), 1)
    lane_of = ((i >> shift) & 3) * nv + (i >> (shift + 2))
    fold[...] = jnp.where(lane_of == j, 1.0, 0.0).astype(BF16)
    load_f.wait()

    mask = same_block(rows, chunk, 2 * nb)
    left = fields[...]
    total = jnp.zeros((rows, 128), F32)
    for load, part in zip(load_v, pieces):
        load.wait()
        grid = jnp.where(mask, dot(left, vectors[part, :], NT), 0.0)
        high = grid.astype(BF16)
        low = (grid - high.astype(F32)).astype(BF16)
        both = dot(jnp.concatenate([high, low], axis=0), fold[part, :], NN)
        total = total + (both[:rows] + both[rows:])
    lane = lax.broadcasted_iota(jnp.int32, (nb, 128), 1)
    sign = jnp.where(lane < 64, 1.0, -1.0)
    for r in range(nr):
        block = [total[(r * 4 + q) * nb:(r * 4 + q + 1) * nb] for q in range(4)]
        coarse = sign * (block[0] + block[1]) + pltpu.roll(block[2] + block[3], 64, 1)
        for x in range(nx):
            ext[x + 1, r * ny:(r + 1) * ny, :] = coarse[x * ny:(x + 1) * ny]
        ext[0, r * ny:(r + 1) * ny, :] = coarse[(nx - 1) * ny:]
        ext[nx + 1, r * ny:(r + 1) * ny, :] = coarse[:ny]

    pl.semaphore_wait(barrier, 3 * nx - 1)
    sends_x, sends_z = [], []
    for d in range(nx):
        other = lax.rem(me + d, nx)
        for side, plane in ((1, up), (0, down)):
            sends_z.append(
                pltpu.make_async_remote_copy(
                    src_ref=ext.at[other + 1],
                    dst_ref=recvz.at[side, me],
                    send_sem=sendz.at[side, d],
                    recv_sem=recvz_sem.at[side, d],
                    device_id=(other, plane, col),
                    device_id_type=MESH,
                )
            )
            sends_z[-1].start()
        if d > 0:
            sends_x.append(
                pltpu.make_async_remote_copy(
                    src_ref=ext.at[pl.ds(other, 3)],
                    dst_ref=recv.at[me],
                    send_sem=send1.at[d],
                    recv_sem=recv1.at[d],
                    device_id=(other, z, col),
                    device_id_type=MESH,
                )
            )
            sends_x[-1].start()
    recv[pl.ds(me, 1)] = ext[pl.ds(me, 3)][None]

    i = lax.broadcasted_iota(jnp.int32, (128, vec_rows), 1)
    j = lax.broadcasted_iota(jnp.int32, (128, vec_rows), 0)
    lane_of = ((i >> shift) & 3) * nv + (i >> (shift + 2))
    spread[...] = jnp.where(lane_of == j, 1.0, 0.0).astype(BF16)

    load_o.wait()
    lane = lax.broadcasted_iota(jnp.int32, (64, 128), 1)
    sign64 = jnp.where(lane < 64, 1.0, -1.0)
    for t in range(nt):
        for y in range(ny):
            for place, m in enumerate(ORDER):
                a = ops[t * ny + y, m].astype(F32)
                both = jnp.concatenate([a * sign64, pltpu.roll(a, 64, 1)], axis=0)
                matrix[t, place * 128:(place + 1) * 128, y * 128:(y + 1) * 128] = both.T.astype(BF16)

    site = lax.broadcasted_iota(jnp.int32, (nr * ny, 128), 0)

    def roll_y(v, step):
        pieces = []
        for r in range(nr):
            for y in range(ny):
                row = r * ny + (y + step) % ny
                pieces.append(v[row:row + 1])
        return jnp.concatenate(pieces, axis=0)

    def product(t, first, terms):
        around = jnp.concatenate(terms, axis=1).astype(BF16)
        return dot(around, matrix[t, first * 128:(first + len(terms)) * 128, :], NN)

    def near(own):
        return [
            product(
                t,
                0,
                [own[t], roll_y(own[t], 1), roll_y(own[t], -1), own[(t + 1) % nt], own[(t - 1) % nt]],
            )
            for t in range(nt)
        ]

    def beside(total, first, plus, minus):
        return [total[t] + product(t, first, [plus[t], minus[t]]) for t in range(nt)]

    def picked(total):
        results = []
        for t in range(nt):
            value = total[t][:, :128]
            for y in range(1, ny):
                value = jnp.where(
                    lax.rem(site, ny) == y, total[t][:, y * 128:(y + 1) * 128], value
                )
            results.append(value.astype(BF16).astype(F32))
        return results

    def summed(load):
        results = []
        for t in range(nt):
            value = load(t * TSITES)
            for s in range(1, TSITES):
                value = value + load(t * TSITES + s)
            results.append(value.astype(BF16).astype(F32))
        return results

    for copy in sends_x:
        copy.wait_recv()
    total = near(summed(lambda s: recv[s, 1]))
    total = beside(total, 5, summed(lambda s: recv[s, 2]), summed(lambda s: recv[s, 0]))
    for copy in sends_z:
        copy.wait_recv()
    applied = picked(
        beside(total, 7, summed(lambda s: recvz[0, s]), summed(lambda s: recvz[1, s]))
    )
    for t in range(nt):
        mine[t] = applied[t]

    right = lax.rem(me + 1, nx)
    left_x = lax.rem(me + nx - 1, nx)
    places = ((3, (me, up)), (2, (me, down)), (1, (right, z)), (0, (left_x, z)))
    round2 = []
    for slot, place in places:
        round2.append(
            pltpu.make_async_remote_copy(
                src_ref=mine,
                dst_ref=halo.at[slot],
                send_sem=send2.at[slot],
                recv_sem=recv2.at[slot],
                device_id=place + (col,),
                device_id_type=MESH,
            )
        )
        round2[-1].start()
    total = near(applied)
    arrived = lambda slot: [halo[slot, t] for t in range(nt)]
    for copy in round2[2:]:
        copy.wait_recv()
    total = beside(total, 5, arrived(0), arrived(1))
    for copy in round2[:2]:
        copy.wait_recv()
    twice = picked(beside(total, 7, arrived(2), arrived(3)))
    for t in range(nt):
        final[t] = twice[t]

    round3 = []
    for d in range(1, nx):
        other = lax.rem(me + d, nx)
        round3.append(
            pltpu.make_async_remote_copy(
                src_ref=final.at[other // TSITES],
                dst_ref=gath.at[me],
                send_sem=send3.at[d],
                recv_sem=recv3.at[d],
                device_id=(other, z, col),
                device_id_type=MESH,
            )
        )
        round3[-1].start()
    gath[pl.ds(me, 1)] = final[pl.ds(me // TSITES, 1)]
    for copy in sends_x + sends_z + round2:
        copy.wait_send()
    for copy in round3:
        copy.wait_recv()

    mixings = []
    for r in range(nr):
        row = jnp.concatenate([gath[x, r * ny:(r + 1) * ny, :] for x in range(nx)], axis=0)
        real = sign * row
        imag = pltpu.roll(row, 64, 1)
        mixings += [real, real, imag, imag]
    mixing = jnp.concatenate(mixings, axis=0).astype(BF16)
    result = None
    for part in pieces:
        weights = jnp.where(mask, dot(mixing, spread[:, part], NN), 0.0).astype(BF16)
        term = dot(weights, vectors[part, :], NN)
        result = term if result is None else result + term
    out_ref[...] = result
    for copy in round3:
        copy.wait_send()


def per_device(right_sides, null_vectors, coarse_op):
    nx = lax.axis_size("ta")
    nz = lax.axis_size("gz")
    nt, ny = coarse_op.shape[2:4]
    nr = right_sides.shape[0]
    nv = null_vectors.shape[0]
    nb, width = null_vectors.shape[-2:]
    vec_rows = nv * 4 * nb
    rows = nr * 4 * nb
    chunk = vec_rows // 4
    message = (nr * ny, 128)
    dma = pltpu.SemaphoreType.DMA
    vectors = null_vectors.reshape(vec_rows, width)
    out = pl.pallas_call(
        functools.partial(kernel, (nx, nz, nt, ny, nr, nv, nb, chunk)),
        out_shape=pltpu.VMEM((rows, width), F32),
        in_specs=[pl.BlockSpec(memory_space=pl.ANY)] * 3,
        out_specs=pl.BlockSpec(memory_space=pltpu.VMEM),
        scratch_shapes=[
            pltpu.VMEM((rows, width), BF16),
            pltpu.VMEM((vec_rows, width), BF16),
            pltpu.VMEM((nt * ny, 9, 64, 128), BF16),
            pltpu.VMEM((vec_rows, 128), BF16),
            pltpu.VMEM((nx + 2,) + message, F32),
            pltpu.VMEM((nt, 9 * 128, ny * 128), BF16),
            pltpu.VMEM((nx, 3) + message, F32),
            pltpu.VMEM((2, nx) + message, F32),
            pltpu.VMEM((nt,) + message, F32),
            pltpu.VMEM((4, nt) + message, F32),
            pltpu.VMEM((nt,) + message, F32),
            pltpu.VMEM((nx,) + message, F32),
            pltpu.VMEM((128, vec_rows), BF16),
            dma((2 + vec_rows // chunk,)),
            dma((nx,)),
            dma((nx,)),
            dma((2, nx)),
            dma((2, nx)),
            dma((4,)),
            dma((4,)),
            dma((nx,)),
            dma((nx,)),
        ],
        compiler_params=pltpu.CompilerParams(
            collective_id=0, has_side_effects=True, vmem_limit_bytes=62 * 1024 * 1024
        ),
    )(
        right_sides.reshape(rows, width),
        vectors,
        coarse_op.reshape((nt * ny,) + coarse_op.shape[4:]),
    )
    return out.reshape(right_sides.shape)


def solution(mesh):
    return jax.shard_map(
        per_device,
        mesh=mesh,
        in_specs=(
            P("col", None, None, "ta", "gz", None, None),
            P(None, None, None, "ta", "gz", None, None),
            P("ta", "gz", None, None, None, None, None),
        ),
        out_specs=P("col", None, None, "ta", "gz", None, None),
        check_vma=False,
    )
```

```python
import functools

import jax
import jax.numpy as jnp
from jax import lax
from jax.experimental import pallas as pl
from jax.experimental.pallas import tpu as pltpu
from jax.sharding import PartitionSpec as P

TSITES = 4
MESH = pl.DeviceIdType.MESH
F32 = jnp.float32
BF16 = jnp.bfloat16
NN = (((1,), (0,)), ((), ()))
NT = (((1,), (1,)), ((), ()))
ORDER = (0, 3, 4, 7, 8, 1, 2, 5, 6)


def dot(a, b, dims):
    return lax.dot_general(a, b, dims, preferred_element_type=F32)


def same_block(rows, lanes, row_period):
    i = lax.broadcasted_iota(jnp.int32, (rows, lanes), 0)
    j = lax.broadcasted_iota(jnp.int32, (rows, lanes), 1)
    return ((i ^ j) & (row_period - 1)) == 0


def kernel(
    dims, fields_hbm, vectors_hbm, ops_hbm, out_ref,
    fields, vectors, ops, ext, matrix, recv, recvz, mine, halo, final, gath, spread,
    load_sem, send1, recv1, sendz, recvz_sem, send2, recv2, send3, recv3,
):
    nx, nz, nt, ny, nr, nv, nb, chunk = dims
    me = lax.axis_index("ta")
    z = lax.axis_index("gz")
    col = lax.axis_index("col")
    up = lax.rem(z + 1, nz)
    down = lax.rem(z + nz - 1, nz)
    shift = nb.bit_length() - 1
    vec_rows = vectors.shape[0]
    rows = fields.shape[0]

    barrier = pltpu.get_barrier_semaphore()
    for d in [*range(1, nx), 0]:
        other = lax.rem(me + d, nx)
        for plane in (up, down) if d == 0 else (up, down, z):
            pl.semaphore_signal(
                barrier, inc=1, device_id=(other, plane, col), device_id_type=MESH
            )

    load_f = pltpu.make_async_copy(fields_hbm, fields, load_sem.at[0])
    pieces = [pl.ds(c * chunk, chunk) for c in range(vectors.shape[0] // chunk)]
    load_v = [
        pltpu.make_async_copy(vectors_hbm.at[part], vectors.at[part], load_sem.at[2 + c])
        for c, part in enumerate(pieces)
    ]
    load_o = pltpu.make_async_copy(ops_hbm, ops, load_sem.at[1])
    load_f.start()
    for load in load_v:
        load.start()
    load_o.start()

    i = lax.broadcasted_iota(jnp.int32, (128, vec_rows), 1)
    j = lax.broadcasted_iota(jnp.int32, (128, vec_rows), 0)
    lane_of = ((i >> shift) & 3) * nv + (i >> (shift + 2))
    spread[...] = jnp.where(lane_of == j, 1.0, 0.0).astype(BF16)
    lane = lax.broadcasted_iota(jnp.int32, (chunk, 2 * rows), 1)
    high_half = lane < rows
    mask_t = same_block(chunk, 2 * rows, 2 * nb)

    load_f.wait()

    left = jnp.concatenate([fields[...], fields[...]], axis=0)
    total = jnp.zeros((128, 2 * rows), F32)
    for load, part in zip(load_v, pieces):
        load.wait()
        grid = jnp.where(mask_t, dot(vectors[part, :], left, NT), 0.0)
        high = grid.astype(BF16)
        low = (grid - high.astype(F32)).astype(BF16)
        total = total + dot(spread[:, part], jnp.where(high_half, high, low), NN)
    total = total.T
    total = total[:rows] + total[rows:]
    lane = lax.broadcasted_iota(jnp.int32, (nb, 128), 1)
    sign = jnp.where(lane < 64, 1.0, -1.0)
    for r in range(nr):
        block = [total[(r * 4 + q) * nb:(r * 4 + q + 1) * nb] for q in range(4)]
        coarse = sign * (block[0] + block[1]) + pltpu.roll(block[2] + block[3], 64, 1)
        for x in range(nx):
            ext[x + 1, r * ny:(r + 1) * ny, :] = coarse[x * ny:(x + 1) * ny]
        ext[0, r * ny:(r + 1) * ny, :] = coarse[(nx - 1) * ny:]
        ext[nx + 1, r * ny:(r + 1) * ny, :] = coarse[:ny]

    pl.semaphore_wait(barrier, 3 * nx - 1)
    sends_x, sends_z = [], []
    for d in [*range(1, nx), 0]:
        other = lax.rem(me + d, nx)
        for side, plane in ((1, up), (0, down)):
            sends_z.append(
                pltpu.make_async_remote_copy(
                    src_ref=ext.at[other + 1],
                    dst_ref=recvz.at[side, me],
                    send_sem=sendz.at[side, d],
                    recv_sem=recvz_sem.at[side, d],
                    device_id=(other, plane, col),
                    device_id_type=MESH,
                )
            )
            sends_z[-1].start()
        if d > 0:
            sends_x.append(
                pltpu.make_async_remote_copy(
                    src_ref=ext.at[pl.ds(other, 3)],
                    dst_ref=recv.at[me],
                    send_sem=send1.at[d],
                    recv_sem=recv1.at[d],
                    device_id=(other, z, col),
                    device_id_type=MESH,
                )
            )
            sends_x[-1].start()
    recv[pl.ds(me, 1)] = ext[pl.ds(me, 3)][None]

    load_o.wait()
    lane = lax.broadcasted_iota(jnp.int32, (64, 128), 1)
    sign64 = jnp.where(lane < 64, 1.0, -1.0)
    for t in range(nt):
        for y in range(ny):
            for place, m in enumerate(ORDER):
                a = ops[t * ny + y, m].astype(F32)
                both = jnp.concatenate([a * sign64, pltpu.roll(a, 64, 1)], axis=0)
                matrix[t, place * 128:(place + 1) * 128, y * 128:(y + 1) * 128] = both.T.astype(BF16)

    site = lax.broadcasted_iota(jnp.int32, (nr * ny, 128), 0)

    def roll_y(v, step):
        pieces = []
        for r in range(nr):
            for y in range(ny):
                row = r * ny + (y + step) % ny
                pieces.append(v[row:row + 1])
        return jnp.concatenate(pieces, axis=0)

    def product(t, first, terms):
        around = jnp.concatenate(terms, axis=1).astype(BF16)
        return dot(around, matrix[t, first * 128:(first + len(terms)) * 128, :], NN)

    def near(own):
        return [
            product(
                t,
                0,
                [own[t], roll_y(own[t], 1), roll_y(own[t], -1), own[(t + 1) % nt], own[(t - 1) % nt]],
            )
            for t in range(nt)
        ]

    def beside(total, first, plus, minus):
        return [total[t] + product(t, first, [plus[t], minus[t]]) for t in range(nt)]

    def picked(total):
        results = []
        for t in range(nt):
            value = total[t][:, :128]
            for y in range(1, ny):
                value = jnp.where(
                    lax.rem(site, ny) == y, total[t][:, y * 128:(y + 1) * 128], value
                )
            results.append(value.astype(BF16).astype(F32))
        return results

    def summed(load):
        results = []
        for t in range(nt):
            value = load(t * TSITES)
            for s in range(1, TSITES):
                value = value + load(t * TSITES + s)
            results.append(value.astype(BF16).astype(F32))
        return results

    for copy in sends_x:
        copy.wait_recv()
    total = near(summed(lambda s: recv[s, 1]))
    total = beside(total, 5, summed(lambda s: recv[s, 2]), summed(lambda s: recv[s, 0]))
    for copy in sends_z:
        copy.wait_recv()
    applied = picked(
        beside(total, 7, summed(lambda s: recvz[0, s]), summed(lambda s: recvz[1, s]))
    )
    for t in range(nt):
        mine[t] = applied[t]

    right = lax.rem(me + 1, nx)
    left_x = lax.rem(me + nx - 1, nx)
    places = ((3, (me, up)), (2, (me, down)), (1, (right, z)), (0, (left_x, z)))
    round2 = []
    for slot, place in places:
        round2.append(
            pltpu.make_async_remote_copy(
                src_ref=mine,
                dst_ref=halo.at[slot],
                send_sem=send2.at[slot],
                recv_sem=recv2.at[slot],
                device_id=place + (col,),
                device_id_type=MESH,
            )
        )
        round2[-1].start()
    total = near(applied)
    arrived = lambda slot: [halo[slot, t] for t in range(nt)]
    for copy in round2[2:]:
        copy.wait_recv()
    total = beside(total, 5, arrived(0), arrived(1))
    for copy in round2[:2]:
        copy.wait_recv()
    twice = picked(beside(total, 7, arrived(2), arrived(3)))
    for t in range(nt):
        final[t] = twice[t]

    round3 = []
    for d in range(1, nx):
        other = lax.rem(me + d, nx)
        round3.append(
            pltpu.make_async_remote_copy(
                src_ref=final.at[other // TSITES],
                dst_ref=gath.at[me],
                send_sem=send3.at[d],
                recv_sem=recv3.at[d],
                device_id=(other, z, col),
                device_id_type=MESH,
            )
        )
        round3[-1].start()
    gath[pl.ds(me, 1)] = final[pl.ds(me // TSITES, 1)]
    for copy in sends_x + sends_z + round2:
        copy.wait_send()
    for copy in round3:
        copy.wait_recv()

    mask = same_block(rows, chunk, 2 * nb)
    mixings = []
    for r in range(nr):
        row = jnp.concatenate([gath[x, r * ny:(r + 1) * ny, :] for x in range(nx)], axis=0)
        real = sign * row
        imag = pltpu.roll(row, 64, 1)
        mixings += [real, real, imag, imag]
    mixing = jnp.concatenate(mixings, axis=0).astype(BF16)
    result = None
    for part in pieces:
        weights = jnp.where(mask, dot(mixing, spread[:, part], NN), 0.0).astype(BF16)
        term = dot(weights, vectors[part, :], NN)
        result = term if result is None else result + term
    out_ref[...] = result
    for copy in round3:
        copy.wait_send()


def per_device(right_sides, null_vectors, coarse_op):
    nx = lax.axis_size("ta")
    nz = lax.axis_size("gz")
    nt, ny = coarse_op.shape[2:4]
    nr = right_sides.shape[0]
    nv = null_vectors.shape[0]
    nb, width = null_vectors.shape[-2:]
    vec_rows = nv * 4 * nb
    rows = nr * 4 * nb
    chunk = min(vec_rows // 2, 1024)
    message = (nr * ny, 128)
    dma = pltpu.SemaphoreType.DMA
    vectors = null_vectors.reshape(vec_rows, width)
    out = pl.pallas_call(
        functools.partial(kernel, (nx, nz, nt, ny, nr, nv, nb, chunk)),
        out_shape=pltpu.VMEM((rows, width), F32),
        in_specs=[pl.BlockSpec(memory_space=pl.ANY)] * 3,
        out_specs=pl.BlockSpec(memory_space=pltpu.VMEM),
        scratch_shapes=[
            pltpu.VMEM((rows, width), BF16),
            pltpu.VMEM((vec_rows, width), BF16),
            pltpu.VMEM((nt * ny, 9, 64, 128), BF16),
            pltpu.VMEM((nx + 2,) + message, F32),
            pltpu.VMEM((nt, 9 * 128, ny * 128), BF16),
            pltpu.VMEM((nx, 3) + message, F32),
            pltpu.VMEM((2, nx) + message, F32),
            pltpu.VMEM((nt,) + message, F32),
            pltpu.VMEM((4, nt) + message, F32),
            pltpu.VMEM((nt,) + message, F32),
            pltpu.VMEM((nx,) + message, F32),
            pltpu.VMEM((128, vec_rows), BF16),
            dma((2 + vec_rows // chunk,)),
            dma((nx,)),
            dma((nx,)),
            dma((2, nx)),
            dma((2, nx)),
            dma((4,)),
            dma((4,)),
            dma((nx,)),
            dma((nx,)),
        ],
        compiler_params=pltpu.CompilerParams(
            collective_id=0, has_side_effects=True, vmem_limit_bytes=62 * 1024 * 1024
        ),
    )(
        right_sides.reshape(rows, width),
        vectors,
        coarse_op.reshape((nt * ny,) + coarse_op.shape[4:]),
    )
    return out.reshape(right_sides.shape)


def solution(mesh):
    return jax.shard_map(
        per_device,
        mesh=mesh,
        in_specs=(
            P("col", None, None, "ta", "gz", None, None),
            P(None, None, None, "ta", "gz", None, None),
            P("ta", "gz", None, None, None, None, None),
        ),
        out_specs=P("col", None, None, "ta", "gz", None, None),
        check_vma=False,
    )
```

```python
import functools

import jax
import jax.numpy as jnp
from jax import lax
from jax.experimental import pallas as pl
from jax.experimental.pallas import tpu as pltpu
from jax.sharding import PartitionSpec as P

TSITES = 4
MESH = pl.DeviceIdType.MESH
F32 = jnp.float32
BF16 = jnp.bfloat16
NN = (((1,), (0,)), ((), ()))
NT = (((1,), (1,)), ((), ()))
ORDER = (0, 3, 4, 7, 8, 1, 2, 5, 6)


def dot(a, b, dims):
    return lax.dot_general(a, b, dims, preferred_element_type=F32)


def same_block(rows, lanes, row_period):
    i = lax.broadcasted_iota(jnp.int32, (rows, lanes), 0)
    j = lax.broadcasted_iota(jnp.int32, (rows, lanes), 1)
    return ((i ^ j) & (row_period - 1)) == 0


def kernel(
    dims, fields_hbm, vectors_hbm, ops_hbm, out_ref,
    fields, vectors, ops, ext, matrix, recv, recvz, mine, halo, final, gath, spread,
    load_sem, send1, recv1, sendz, recvz_sem, send2, recv2, send3, recv3,
):
    nx, nz, nt, ny, nr, nv, nb, chunk = dims
    me = lax.axis_index("ta")
    z = lax.axis_index("gz")
    col = lax.axis_index("col")
    up = lax.rem(z + 1, nz)
    down = lax.rem(z + nz - 1, nz)
    shift = nb.bit_length() - 1
    vec_rows = vectors.shape[0]
    rows = fields.shape[0]

    barrier = pltpu.get_barrier_semaphore()
    for d in [*range(1, nx), 0]:
        other = lax.rem(me + d, nx)
        for plane in (up, down) if d == 0 else (up, down, z):
            pl.semaphore_signal(
                barrier, inc=1, device_id=(other, plane, col), device_id_type=MESH
            )

    load_f = pltpu.make_async_copy(fields_hbm, fields, load_sem.at[0])
    pieces = [pl.ds(c * chunk, chunk) for c in range(vectors.shape[0] // chunk)]
    load_v = [
        pltpu.make_async_copy(vectors_hbm.at[part], vectors.at[part], load_sem.at[2 + c])
        for c, part in enumerate(pieces)
    ]
    load_o = pltpu.make_async_copy(ops_hbm, ops, load_sem.at[1])
    load_f.start()
    for load in load_v:
        load.start()
    load_o.start()

    i = lax.broadcasted_iota(jnp.int32, (128, vec_rows), 1)
    j = lax.broadcasted_iota(jnp.int32, (128, vec_rows), 0)
    lane_of = ((i >> shift) & 3) * nv + (i >> (shift + 2))
    spread[...] = jnp.where(lane_of == j, 1.0, 0.0).astype(BF16)
    lane = lax.broadcasted_iota(jnp.int32, (chunk, 2 * rows), 1)
    high_half = lane < rows
    mask_t = same_block(chunk, 2 * rows, 2 * nb)

    load_f.wait()

    left = jnp.concatenate([fields[...], fields[...]], axis=0)
    total = jnp.zeros((128, 2 * rows), F32)
    for load, part in zip(load_v, pieces):
        load.wait()
        grid = jnp.where(mask_t, dot(vectors[part, :], left, NT), 0.0)
        high = grid.astype(BF16)
        low = (grid - high.astype(F32)).astype(BF16)
        total = total + dot(spread[:, part], jnp.where(high_half, high, low), NN)
    total = total.T
    total = total[:rows] + total[rows:]
    lane = lax.broadcasted_iota(jnp.int32, (nb, 128), 1)
    sign = jnp.where(lane < 64, 1.0, -1.0)
    for r in range(nr):
        block = [total[(r * 4 + q) * nb:(r * 4 + q + 1) * nb] for q in range(4)]
        coarse = sign * (block[0] + block[1]) + pltpu.roll(block[2] + block[3], 64, 1)
        for x in range(nx):
            ext[x + 1, r * ny:(r + 1) * ny, :] = coarse[x * ny:(x + 1) * ny]
        ext[0, r * ny:(r + 1) * ny, :] = coarse[(nx - 1) * ny:]
        ext[nx + 1, r * ny:(r + 1) * ny, :] = coarse[:ny]

    pl.semaphore_wait(barrier, 3 * nx - 1)
    sends_x, sends_z = [], []
    for d in [*range(1, nx), 0]:
        other = lax.rem(me + d, nx)
        for side, plane in ((1, up), (0, down)):
            sends_z.append(
                pltpu.make_async_remote_copy(
                    src_ref=ext.at[other + 1],
                    dst_ref=recvz.at[side, me],
                    send_sem=sendz.at[0],
                    recv_sem=recvz_sem.at[0],
                    device_id=(other, plane, col),
                    device_id_type=MESH,
                )
            )
            sends_z[-1].start()
        if d > 0:
            sends_x.append(
                pltpu.make_async_remote_copy(
                    src_ref=ext.at[pl.ds(other, 3)],
                    dst_ref=recv.at[me],
                    send_sem=send1.at[0],
                    recv_sem=recv1.at[0],
                    device_id=(other, z, col),
                    device_id_type=MESH,
                )
            )
            sends_x[-1].start()
    recv[pl.ds(me, 1)] = ext[pl.ds(me, 3)][None]

    load_o.wait()
    lane = lax.broadcasted_iota(jnp.int32, (64, 128), 1)
    sign64 = jnp.where(lane < 64, 1.0, -1.0)
    for t in range(nt):
        for y in range(ny):
            for place, m in enumerate(ORDER):
                a = ops[t * ny + y, m].astype(F32)
                both = jnp.concatenate([a * sign64, pltpu.roll(a, 64, 1)], axis=0)
                matrix[t, place * 128:(place + 1) * 128, y * 128:(y + 1) * 128] = both.T.astype(BF16)

    site = lax.broadcasted_iota(jnp.int32, (nr * ny, 128), 0)

    def roll_y(v, step):
        pieces = []
        for r in range(nr):
            for y in range(ny):
                row = r * ny + (y + step) % ny
                pieces.append(v[row:row + 1])
        return jnp.concatenate(pieces, axis=0)

    def product(t, first, terms):
        around = jnp.concatenate(terms, axis=1).astype(BF16)
        return dot(around, matrix[t, first * 128:(first + len(terms)) * 128, :], NN)

    def near(own):
        return [
            product(
                t,
                0,
                [own[t], roll_y(own[t], 1), roll_y(own[t], -1), own[(t + 1) % nt], own[(t - 1) % nt]],
            )
            for t in range(nt)
        ]

    def beside(total, first, plus, minus):
        return [total[t] + product(t, first, [plus[t], minus[t]]) for t in range(nt)]

    def picked(total):
        results = []
        for t in range(nt):
            value = total[t][:, :128]
            for y in range(1, ny):
                value = jnp.where(
                    lax.rem(site, ny) == y, total[t][:, y * 128:(y + 1) * 128], value
                )
            results.append(value.astype(BF16).astype(F32))
        return results

    def summed(load):
        results = []
        for t in range(nt):
            value = load(t * TSITES)
            for s in range(1, TSITES):
                value = value + load(t * TSITES + s)
            results.append(value.astype(BF16).astype(F32))
        return results

    others = recv.at[pl.ds(0, nx - 1)]
    pltpu.make_async_copy(others, others, recv1.at[0]).wait()
    total = near(summed(lambda s: recv[s, 1]))
    total = beside(total, 5, summed(lambda s: recv[s, 2]), summed(lambda s: recv[s, 0]))
    pltpu.make_async_copy(recvz, recvz, recvz_sem.at[0]).wait()
    applied = picked(
        beside(total, 7, summed(lambda s: recvz[0, s]), summed(lambda s: recvz[1, s]))
    )
    for t in range(nt):
        mine[t] = applied[t]

    right = lax.rem(me + 1, nx)
    left_x = lax.rem(me + nx - 1, nx)
    places = ((3, (me, up)), (2, (me, down)), (1, (right, z)), (0, (left_x, z)))
    round2 = []
    for slot, place in places:
        round2.append(
            pltpu.make_async_remote_copy(
                src_ref=mine,
                dst_ref=halo.at[slot],
                send_sem=send2.at[slot],
                recv_sem=recv2.at[slot],
                device_id=place + (col,),
                device_id_type=MESH,
            )
        )
        round2[-1].start()
    total = near(applied)
    arrived = lambda slot: [halo[slot, t] for t in range(nt)]
    for copy in round2[2:]:
        copy.wait_recv()
    total = beside(total, 5, arrived(0), arrived(1))
    for copy in round2[:2]:
        copy.wait_recv()
    twice = picked(beside(total, 7, arrived(2), arrived(3)))
    for t in range(nt):
        final[t] = twice[t]

    round3 = []
    for d in range(1, nx):
        other = lax.rem(me + d, nx)
        round3.append(
            pltpu.make_async_remote_copy(
                src_ref=final.at[other // TSITES],
                dst_ref=gath.at[me],
                send_sem=send3.at[d],
                recv_sem=recv3.at[d],
                device_id=(other, z, col),
                device_id_type=MESH,
            )
        )
        round3[-1].start()
    gath[pl.ds(me, 1)] = final[pl.ds(me // TSITES, 1)]
    pltpu.make_async_copy(others, others, send1.at[0]).wait()
    pltpu.make_async_copy(recvz, recvz, sendz.at[0]).wait()
    for copy in round2:
        copy.wait_send()
    for copy in round3:
        copy.wait_recv()

    mask = same_block(rows, chunk, 2 * nb)
    mixings = []
    for r in range(nr):
        row = jnp.concatenate([gath[x, r * ny:(r + 1) * ny, :] for x in range(nx)], axis=0)
        real = sign * row
        imag = pltpu.roll(row, 64, 1)
        mixings += [real, real, imag, imag]
    mixing = jnp.concatenate(mixings, axis=0).astype(BF16)
    result = None
    for part in pieces:
        weights = jnp.where(mask, dot(mixing, spread[:, part], NN), 0.0).astype(BF16)
        term = dot(weights, vectors[part, :], NN)
        result = term if result is None else result + term
    out_ref[...] = result
    for copy in round3:
        copy.wait_send()


def per_device(right_sides, null_vectors, coarse_op):
    nx = lax.axis_size("ta")
    nz = lax.axis_size("gz")
    nt, ny = coarse_op.shape[2:4]
    nr = right_sides.shape[0]
    nv = null_vectors.shape[0]
    nb, width = null_vectors.shape[-2:]
    vec_rows = nv * 4 * nb
    rows = nr * 4 * nb
    chunk = min(vec_rows // 2, 1024)
    message = (nr * ny, 128)
    dma = pltpu.SemaphoreType.DMA
    vectors = null_vectors.reshape(vec_rows, width)
    out = pl.pallas_call(
        functools.partial(kernel, (nx, nz, nt, ny, nr, nv, nb, chunk)),
        out_shape=pltpu.VMEM((rows, width), F32),
        in_specs=[pl.BlockSpec(memory_space=pl.ANY)] * 3,
        out_specs=pl.BlockSpec(memory_space=pltpu.VMEM),
        scratch_shapes=[
            pltpu.VMEM((rows, width), BF16),
            pltpu.VMEM((vec_rows, width), BF16),
            pltpu.VMEM((nt * ny, 9, 64, 128), BF16),
            pltpu.VMEM((nx + 2,) + message, F32),
            pltpu.VMEM((nt, 9 * 128, ny * 128), BF16),
            pltpu.VMEM((nx, 3) + message, F32),
            pltpu.VMEM((2, nx) + message, F32),
            pltpu.VMEM((nt,) + message, F32),
            pltpu.VMEM((4, nt) + message, F32),
            pltpu.VMEM((nt,) + message, F32),
            pltpu.VMEM((nx,) + message, F32),
            pltpu.VMEM((128, vec_rows), BF16),
            dma((2 + vec_rows // chunk,)),
            dma((1,)),
            dma((1,)),
            dma((1,)),
            dma((1,)),
            dma((4,)),
            dma((4,)),
            dma((nx,)),
            dma((nx,)),
        ],
        compiler_params=pltpu.CompilerParams(
            collective_id=0, has_side_effects=True, vmem_limit_bytes=62 * 1024 * 1024
        ),
    )(
        right_sides.reshape(rows, width),
        vectors,
        coarse_op.reshape((nt * ny,) + coarse_op.shape[4:]),
    )
    return out.reshape(right_sides.shape)


def solution(mesh):
    return jax.shard_map(
        per_device,
        mesh=mesh,
        in_specs=(
            P("col", None, None, "ta", "gz", None, None),
            P(None, None, None, "ta", "gz", None, None),
            P("ta", "gz", None, None, None, None, None),
        ),
        out_specs=P("col", None, None, "ta", "gz", None, None),
        check_vma=False,
    )
```

```python
import functools

import jax
import jax.numpy as jnp
from jax import lax
from jax.experimental import pallas as pl
from jax.experimental.pallas import tpu as pltpu
from jax.sharding import PartitionSpec as P

TSITES = 4
MESH = pl.DeviceIdType.MESH
F32 = jnp.float32
BF16 = jnp.bfloat16
NN = (((1,), (0,)), ((), ()))
NT = (((1,), (1,)), ((), ()))
ORDER = (0, 3, 4, 7, 8, 1, 2, 5, 6)


def dot(a, b, dims):
    return lax.dot_general(a, b, dims, preferred_element_type=F32)


def same_block(rows, lanes, row_period):
    i = lax.broadcasted_iota(jnp.int32, (rows, lanes), 0)
    j = lax.broadcasted_iota(jnp.int32, (rows, lanes), 1)
    return ((i ^ j) & (row_period - 1)) == 0


def kernel(
    dims, fields_hbm, vectors_hbm, ops_hbm, out_ref,
    fields, vectors, ops, ext, matrix, recv, recvz, mine, halo, final, gath, spread,
    load_sem, send1, recv1, sendz, recvz_sem, send2, recv2, send3, recv3,
):
    nx, nz, nt, ny, nr, nv, nb, chunk = dims
    me = lax.axis_index("ta")
    z = lax.axis_index("gz")
    col = lax.axis_index("col")
    up = lax.rem(z + 1, nz)
    down = lax.rem(z + nz - 1, nz)
    shift = nb.bit_length() - 1
    vec_rows = vectors.shape[0]
    rows = fields.shape[0]

    barrier = pltpu.get_barrier_semaphore()
    for d in [*range(1, nx), 0]:
        other = lax.rem(me + d, nx)
        for plane in (up, down) if d == 0 else (up, down, z):
            pl.semaphore_signal(
                barrier, inc=1, device_id=(other, plane, col), device_id_type=MESH
            )

    load_f = pltpu.make_async_copy(fields_hbm, fields, load_sem.at[0])
    pieces = [pl.ds(c * chunk, chunk) for c in range(vectors.shape[0] // chunk)]
    load_v = [
        pltpu.make_async_copy(vectors_hbm.at[part], vectors.at[part], load_sem.at[2 + c])
        for c, part in enumerate(pieces)
    ]
    load_o = pltpu.make_async_copy(ops_hbm, ops, load_sem.at[1])
    load_f.start()
    for load in load_v:
        load.start()
    load_o.start()

    i = lax.broadcasted_iota(jnp.int32, (128, vec_rows), 1)
    j = lax.broadcasted_iota(jnp.int32, (128, vec_rows), 0)
    lane_of = ((i >> shift) & 3) * nv + (i >> (shift + 2))
    spread[...] = jnp.where(lane_of == j, 1.0, 0.0).astype(BF16)
    lane = lax.broadcasted_iota(jnp.int32, (chunk, 2 * rows), 1)
    high_half = lane < rows
    mask_t = same_block(chunk, 2 * rows, 2 * nb)

    load_f.wait()

    left = jnp.concatenate([fields[...], fields[...]], axis=0)
    total = jnp.zeros((128, 2 * rows), F32)
    for load, part in zip(load_v, pieces):
        load.wait()
        grid = jnp.where(mask_t, dot(vectors[part, :], left, NT), 0.0)
        high = grid.astype(BF16)
        low = (grid - high.astype(F32)).astype(BF16)
        total = total + dot(spread[:, part], jnp.where(high_half, high, low), NN)
    total = total.T
    total = total[:rows] + total[rows:]
    lane = lax.broadcasted_iota(jnp.int32, (nb, 128), 1)
    sign = jnp.where(lane < 64, 1.0, -1.0)
    for r in range(nr):
        block = [total[(r * 4 + q) * nb:(r * 4 + q + 1) * nb] for q in range(4)]
        coarse = sign * (block[0] + block[1]) + pltpu.roll(block[2] + block[3], 64, 1)
        for x in range(nx):
            ext[x + 1, r * ny:(r + 1) * ny, :] = coarse[x * ny:(x + 1) * ny]
        ext[0, r * ny:(r + 1) * ny, :] = coarse[(nx - 1) * ny:]
        ext[nx + 1, r * ny:(r + 1) * ny, :] = coarse[:ny]

    pl.semaphore_wait(barrier, 3 * nx - 1)
    sends_x, sends_z = [], []
    for d in [*range(1, nx), 0]:
        other = lax.rem(me + d, nx)
        for side, plane in ((1, up), (0, down)):
            sends_z.append(
                pltpu.make_async_remote_copy(
                    src_ref=ext.at[other + 1],
                    dst_ref=recvz.at[side, me],
                    send_sem=sendz.at[0],
                    recv_sem=recvz_sem.at[0],
                    device_id=(other, plane, col),
                    device_id_type=MESH,
                )
            )
            sends_z[-1].start()
        if d > 0:
            sends_x.append(
                pltpu.make_async_remote_copy(
                    src_ref=ext.at[pl.ds(other, 3)],
                    dst_ref=recv.at[me],
                    send_sem=send1.at[0],
                    recv_sem=recv1.at[0],
                    device_id=(other, z, col),
                    device_id_type=MESH,
                )
            )
            sends_x[-1].start()
    recv[pl.ds(me, 1)] = ext[pl.ds(me, 3)][None]

    load_o.wait()
    lane = lax.broadcasted_iota(jnp.int32, (64, 128), 1)
    sign64 = jnp.where(lane < 64, 1.0, -1.0)
    for t in range(nt):
        for y in range(ny):
            for place, m in enumerate(ORDER):
                a = ops[t * ny + y, m].astype(F32)
                both = jnp.concatenate([a * sign64, pltpu.roll(a, 64, 1)], axis=0)
                matrix[t, place * 128:(place + 1) * 128, y * 128:(y + 1) * 128] = both.T.astype(BF16)

    site = lax.broadcasted_iota(jnp.int32, (nr * ny, 128), 0)

    def roll_y(v, step):
        pieces = []
        for r in range(nr):
            for y in range(ny):
                row = r * ny + (y + step) % ny
                pieces.append(v[row:row + 1])
        return jnp.concatenate(pieces, axis=0)

    def product(t, first, terms):
        around = jnp.concatenate(terms, axis=1).astype(BF16)
        return dot(around, matrix[t, first * 128:(first + len(terms)) * 128, :], NN)

    def near(own):
        return [
            product(
                t,
                0,
                [own[t], roll_y(own[t], 1), roll_y(own[t], -1), own[(t + 1) % nt], own[(t - 1) % nt]],
            )
            for t in range(nt)
        ]

    def beside(total, first, plus, minus):
        return [total[t] + product(t, first, [plus[t], minus[t]]) for t in range(nt)]

    def picked(total):
        results = []
        for t in range(nt):
            value = total[t][:, :128]
            for y in range(1, ny):
                value = jnp.where(
                    lax.rem(site, ny) == y, total[t][:, y * 128:(y + 1) * 128], value
                )
            results.append(value.astype(BF16).astype(F32))
        return results

    def summed(load):
        results = []
        for t in range(nt):
            value = load(t * TSITES)
            for s in range(1, TSITES):
                value = value + load(t * TSITES + s)
            results.append(value.astype(BF16).astype(F32))
        return results

    others = recv.at[pl.ds(0, nx - 1)]
    pltpu.make_async_copy(others, others, recv1.at[0]).wait()
    total = near(summed(lambda s: recv[s, 1]))
    total = beside(total, 5, summed(lambda s: recv[s, 2]), summed(lambda s: recv[s, 0]))
    pltpu.make_async_copy(recvz, recvz, recvz_sem.at[0]).wait()
    applied = picked(
        beside(total, 7, summed(lambda s: recvz[0, s]), summed(lambda s: recvz[1, s]))
    )
    for t in range(nt):
        mine[t] = applied[t]

    right = lax.rem(me + 1, nx)
    left_x = lax.rem(me + nx - 1, nx)
    places = ((3, (me, up)), (2, (me, down)), (1, (right, z)), (0, (left_x, z)))
    round2 = []
    for slot, place in places:
        round2.append(
            pltpu.make_async_remote_copy(
                src_ref=mine,
                dst_ref=halo.at[slot],
                send_sem=send2.at[0],
                recv_sem=recv2.at[slot // 2],
                device_id=place + (col,),
                device_id_type=MESH,
            )
        )
        round2[-1].start()
    total = near(applied)
    arrived = lambda slot: [halo[slot, t] for t in range(nt)]
    pair = halo.at[pl.ds(0, 2)]
    pltpu.make_async_copy(pair, pair, recv2.at[0]).wait()
    total = beside(total, 5, arrived(0), arrived(1))
    pltpu.make_async_copy(pair, pair, recv2.at[1]).wait()
    twice = picked(beside(total, 7, arrived(2), arrived(3)))
    for t in range(nt):
        final[t] = twice[t]

    round3 = []
    for d in range(1, nx):
        other = lax.rem(me + d, nx)
        round3.append(
            pltpu.make_async_remote_copy(
                src_ref=final.at[other // TSITES],
                dst_ref=gath.at[me],
                send_sem=send3.at[0],
                recv_sem=recv3.at[0],
                device_id=(other, z, col),
                device_id_type=MESH,
            )
        )
        round3[-1].start()
    gath[pl.ds(me, 1)] = final[pl.ds(me // TSITES, 1)]
    pltpu.make_async_copy(others, others, send1.at[0]).wait()
    pltpu.make_async_copy(recvz, recvz, sendz.at[0]).wait()
    pltpu.make_async_copy(halo, halo, send2.at[0]).wait()
    rest = gath.at[pl.ds(0, nx - 1)]
    pltpu.make_async_copy(rest, rest, recv3.at[0]).wait()

    mask = same_block(rows, chunk, 2 * nb)
    mixings = []
    for r in range(nr):
        row = jnp.concatenate([gath[x, r * ny:(r + 1) * ny, :] for x in range(nx)], axis=0)
        real = sign * row
        imag = pltpu.roll(row, 64, 1)
        mixings += [real, real, imag, imag]
    mixing = jnp.concatenate(mixings, axis=0).astype(BF16)
    result = None
    for part in pieces:
        weights = jnp.where(mask, dot(mixing, spread[:, part], NN), 0.0).astype(BF16)
        term = dot(weights, vectors[part, :], NN)
        result = term if result is None else result + term
    out_ref[...] = result
    pltpu.make_async_copy(rest, rest, send3.at[0]).wait()


def per_device(right_sides, null_vectors, coarse_op):
    nx = lax.axis_size("ta")
    nz = lax.axis_size("gz")
    nt, ny = coarse_op.shape[2:4]
    nr = right_sides.shape[0]
    nv = null_vectors.shape[0]
    nb, width = null_vectors.shape[-2:]
    vec_rows = nv * 4 * nb
    rows = nr * 4 * nb
    chunk = min(vec_rows // 2, 1024)
    message = (nr * ny, 128)
    dma = pltpu.SemaphoreType.DMA
    vectors = null_vectors.reshape(vec_rows, width)
    out = pl.pallas_call(
        functools.partial(kernel, (nx, nz, nt, ny, nr, nv, nb, chunk)),
        out_shape=pltpu.VMEM((rows, width), F32),
        in_specs=[pl.BlockSpec(memory_space=pl.ANY)] * 3,
        out_specs=pl.BlockSpec(memory_space=pltpu.VMEM),
        scratch_shapes=[
            pltpu.VMEM((rows, width), BF16),
            pltpu.VMEM((vec_rows, width), BF16),
            pltpu.VMEM((nt * ny, 9, 64, 128), BF16),
            pltpu.VMEM((nx + 2,) + message, F32),
            pltpu.VMEM((nt, 9 * 128, ny * 128), BF16),
            pltpu.VMEM((nx, 3) + message, F32),
            pltpu.VMEM((2, nx) + message, F32),
            pltpu.VMEM((nt,) + message, F32),
            pltpu.VMEM((4, nt) + message, F32),
            pltpu.VMEM((nt,) + message, F32),
            pltpu.VMEM((nx,) + message, F32),
            pltpu.VMEM((128, vec_rows), BF16),
            dma((2 + vec_rows // chunk,)),
            dma((1,)),
            dma((1,)),
            dma((1,)),
            dma((1,)),
            dma((1,)),
            dma((2,)),
            dma((1,)),
            dma((1,)),
        ],
        compiler_params=pltpu.CompilerParams(
            collective_id=0, has_side_effects=True, vmem_limit_bytes=62 * 1024 * 1024
        ),
    )(
        right_sides.reshape(rows, width),
        vectors,
        coarse_op.reshape((nt * ny,) + coarse_op.shape[4:]),
    )
    return out.reshape(right_sides.shape)


def solution(mesh):
    return jax.shard_map(
        per_device,
        mesh=mesh,
        in_specs=(
            P("col", None, None, "ta", "gz", None, None),
            P(None, None, None, "ta", "gz", None, None),
            P("ta", "gz", None, None, None, None, None),
        ),
        out_specs=P("col", None, None, "ta", "gz", None, None),
        check_vma=False,
    )
```
